32 devices in a mesh: blk: 8 (over z, core), batch: 2 (over x), tensor: 2 (over y).
Axes of the slice: x: 2, y: 2, z: 4, core: 2. Of those that a mesh axis runs over, the one named last changes fastest.
Arguments:
- queries: bfloat16 [64, 8192], P(('blk', 'batch'), 'tensor'), may hold values from -32 to 32
- new_keys: bfloat16 [64, 1024], P(('blk', 'batch'), 'tensor'), may hold values from -15 to 15
- new_values: bfloat16 [64, 1024], P(('blk', 'batch'), 'tensor'), may hold values from -6 to 6
- suffix_keys: bfloat16 [64, 512, 1024], P(('blk', 'batch'), None, 'tensor'), may hold values from -9 to 9
- suffix_values: bfloat16 [64, 512, 1024], P(('blk', 'batch'), None, 'tensor'), may hold values from -6 to 6
- suffix_lengths: int32 [64], P(('blk', 'batch')), may hold values from 0 to 512, as said below
- prefix_keys: bfloat16 [16384, 1024], P('blk', 'tensor'), may hold values from -6 to 6
- prefix_values: bfloat16 [16384, 1024], P('blk', 'tensor'), may hold values from -6 to 6
- out_weight: bfloat16 [8192, 4096], P('tensor', 'batch'), may hold values from -0.0625 to 0.0625
Outputs:
- projected: bfloat16 [64, 4096], P(('blk', 'tensor'), 'batch')
The draws below stay inside these ranges and needn't reach their ends.
Inputs may be any that keep to these rules, and one draw needn't show every extreme that they name: `suffix_lengths`: some sample has exactly 512 live slots.
All inputs are finite; a program needn't handle non-finite values.
Results may differ from the reference program's by a relative error of at most 0.005.
Values may be sent and summed in bfloat16 or wider, within the bound.
A program may use at most 128 MiB of HBM per device.

```python
import jax
import jax.numpy as jnp
from jax import lax

H = 64
KVH = 8
HD = 128
PREFIX_DEV = 2048
SUF = 512
DW = 4096
S = 64
PREFIX = 16384
N_BLK = 8


def draw_queries(key, part):
    key = jax.random.fold_in(key, 1)
    base_draw = jnp.clip(3.0 * jax.random.normal(key, (S, H * HD), jnp.float32), -18.0, 18.0)
    return base_draw.astype(jnp.bfloat16)


def draw_prefix_keys(key, part):
    key = jax.random.fold_in(key, 2)
    base_draw = jnp.clip(jax.random.normal(key, (PREFIX, KVH * HD), jnp.float32), -6.0, 6.0)
    return base_draw.astype(jnp.bfloat16)


def draw_suffix_lengths(key, part):
    key = jax.random.fold_in(key, 3)
    first_key, second_key, third_key = jax.random.split(key, 3)
    first_draw = jax.random.randint(first_key, (S,), 0, SUF + 1)
    second_draw = jax.random.randint(second_key, (S,), 0, SUF + 1)
    lengths = jnp.minimum(first_draw, second_draw)
    longest = jax.random.randint(third_key, (), 0, S)
    return lengths.at[longest].set(SUF).astype(jnp.int32)


def block_levels(stream_key, dims, cuts, low, top_value):
    loudness, own = 1.0, jax.random.fold_in(stream_key, 6)
    for position, blocks in cuts:
        heights = jnp.exp(jax.random.uniform(jax.random.fold_in(own, position), (blocks,), jnp.float32, low / len(cuts), top_value / len(cuts)))
        loudness = loudness * jnp.repeat(heights, dims[position] // blocks).reshape([-1 if axis == position else 1 for axis in range(len(dims))])
    return loudness


def bell_draw(key, extent, scale, limit, shards=(), held_as=jnp.bfloat16):
    level = block_levels(key, extent, shards, -0.22, 0.18) if shards else 1.0
    result = jax.random.normal(key, extent, jnp.float32) * scale * level
    return jnp.minimum(jnp.maximum(result, -limit), limit).astype(held_as)


def setup_inputs(seed: int = 0) -> dict:
    splits = jax.random.split(jax.random.key(seed), 10)
    queries = draw_queries(jax.random.fold_in(splits[9], 71), 0)
    new_keys = bell_draw(splits[1], (S, KVH * HD), 2.5, 15.0, ((0, 16), (1, 2)))
    new_values = bell_draw(splits[2], (S, KVH * HD), 1.0, 6.0, ((0, 16), (1, 2)))
    suffix_keys = bell_draw(splits[3], (S, SUF, KVH * HD), 1.5, 9.0, ((0, 16), (2, 2)))
    suffix_values = bell_draw(splits[4], (S, SUF, KVH * HD), 1.0, 6.0, ((0, 16), (2, 2)))
    suffix_lengths = draw_suffix_lengths(jax.random.fold_in(splits[9], 71), 0)
    prefix_keys = draw_prefix_keys(jax.random.fold_in(splits[9], 71), 0)
    prefix_values = bell_draw(splits[7], (PREFIX, KVH * HD), 1.0, 6.0, ((0, 8), (1, 2)))
    out_weight = bell_draw(splits[8], (H * HD, DW), (H * HD) ** -0.5, 0.0625, ((0, 2), (1, 2)))
    return {"queries": queries, "new_keys": new_keys, "new_values": new_values, "suffix_keys": suffix_keys, "suffix_values": suffix_values, "suffix_lengths": suffix_lengths, "prefix_keys": prefix_keys, "prefix_values": prefix_values, "out_weight": out_weight}


def reference(queries, new_keys, new_values, suffix_keys, suffix_values, suffix_lengths, prefix_keys, prefix_values, out_weight):
    factor = HD ** -0.5
    groups = H // KVH
    query_heads = queries.reshape(S, KVH, groups, HD).transpose(1, 0, 2, 3)
    prefix_key_heads = prefix_keys.reshape(PREFIX, KVH, HD).transpose(1, 0, 2)
    prefix_value_heads = prefix_values.reshape(PREFIX, KVH, HD).transpose(1, 0, 2)
    suffix_key_heads = suffix_keys.reshape(S, SUF, KVH, HD).transpose(2, 0, 1, 3)
    suffix_value_heads = suffix_values.reshape(S, SUF, KVH, HD).transpose(2, 0, 1, 3)
    new_key_heads = new_keys.reshape(S, KVH, HD).transpose(1, 0, 2)
    new_value_heads = new_values.reshape(S, KVH, HD).transpose(1, 0, 2)
    live_slots = jnp.arange(SUF, dtype=jnp.int32)[None, :] < suffix_lengths[:, None]

    def one_group(operands):
        head_queries, head_prefix_keys, head_prefix_values, head_suffix_keys, head_suffix_values, head_new_keys, head_new_values = operands
        query_float = head_queries.astype(jnp.float32)
        prefix_scores = jnp.einsum("sgd,pd->sgp", query_float, head_prefix_keys.astype(jnp.float32)) * factor
        prefix_scores = prefix_scores.reshape(S, groups, N_BLK, PREFIX_DEV)
        block_top = prefix_scores.max(-1)
        suffix_scores = jnp.einsum("sgd,std->sgt", query_float, head_suffix_keys.astype(jnp.float32)) * factor
        suffix_scores = jnp.where(live_slots[:, None, :], suffix_scores, -jnp.inf)
        own_scores = jnp.einsum("sgd,sd->sg", query_float, head_new_keys.astype(jnp.float32)) * factor
        row_top = jnp.maximum(jnp.maximum(block_top.max(-1), suffix_scores.max(-1)), own_scores)
        prefix_weights = jnp.exp(prefix_scores - block_top[..., None]).astype(jnp.bfloat16)
        suffix_weights = jnp.exp(suffix_scores - row_top[..., None]).astype(jnp.bfloat16)
        own_weights = jnp.exp(own_scores - row_top).astype(jnp.bfloat16)
        prefix_float = lax.optimization_barrier(prefix_weights).astype(jnp.float32)
        suffix_float = lax.optimization_barrier(suffix_weights).astype(jnp.float32)
        own_float = lax.optimization_barrier(own_weights).astype(jnp.float32)
        block_scale = jnp.exp(block_top - row_top[..., None])
        block_mass = prefix_float.sum(-1)
        row_mass = (block_mass * block_scale).sum(-1) + suffix_float.sum(-1) + own_float
        value_blocks = head_prefix_values.astype(jnp.float32).reshape(N_BLK, PREFIX_DEV, HD)
        block_weighted = jnp.einsum("sgbp,bpd->sgbd", prefix_float, value_blocks)
        weighted = jnp.einsum("sgbd,sgb->sgd", block_weighted, block_scale)
        weighted = weighted + jnp.einsum("sgt,std->sgd", suffix_float, head_suffix_values.astype(jnp.float32))
        weighted = weighted + own_float[..., None] * head_new_values.astype(jnp.float32)[:, None, :]
        return (weighted / row_mass[..., None]).astype(jnp.bfloat16)

    attended = lax.map(one_group, (query_heads, prefix_key_heads, prefix_value_heads, suffix_key_heads, suffix_value_heads, new_key_heads, new_value_heads))
    attended = attended.transpose(1, 0, 2, 3).reshape(S, H * HD)
    return jnp.dot(attended, out_weight, preferred_element_type=jnp.float32).astype(jnp.bfloat16)
```

```python
import functools

import jax
import jax.numpy as jnp
from jax import lax
from jax.experimental import pallas as pl
from jax.experimental.pallas import tpu as pltpu
from jax.sharding import PartitionSpec as P

HD = 128
SCALE = HD ** (-0.5)
F32 = jnp.float32
BF16 = jnp.bfloat16
MESH = pl.DeviceIdType.MESH
NT = (((1,), (1,)), ((), ()))
KEY_CHUNK = 512
COL_CHUNK = 256


def head_lanes(k):
    return pl.ds(pl.multiple_of(k * HD, HD), HD)


def kernel(
    nb, nbt, nt, n,
    q_ref, nk_ref, nv_ref, len_ref, sk_hbm, sv_hbm, pk_hbm, pv_hbm, w_hbm,
    o_ref,
    sk, sv, pk, pv, w, qbuf, sbuf, stat, psend, prec, lacc, lm, lmass,
    abuf, a32, x, osend, orecv,
    lsem, q_s, q_r, p_s, p_r, a_s, a_r, o_s, o_r,
):
    kv, rows, _ = q_ref.shape
    groups = rows // n
    slots = sk.shape[1]
    prefix = pk.shape[0]
    me = lax.axis_index("blk")
    mb = lax.axis_index("batch")
    mt = lax.axis_index("tensor")

    loads = [
        pltpu.make_async_copy(src, dst, lsem.at[i])
        for i, (src, dst) in enumerate(
            [(sk_hbm, sk), (sv_hbm, sv), (pk_hbm, pk), (pv_hbm, pv), (w_hbm, w)]
        )
    ]
    for load in loads:
        load.start()

    barrier = pltpu.get_barrier_semaphore()
    for axis, mine, size in (("blk", me, nb), ("batch", mb, nbt), ("tensor", mt, nt)):
        for r in range(1, size):
            pl.semaphore_signal(
                barrier, inc=1, device_id={axis: lax.rem(mine + r, size)}, device_id_type=MESH
            )
    qbuf[:, me] = q_ref[...]
    pl.semaphore_wait(barrier, nb + nbt + nt - 3)

    def q_copy(k, r):
        return pltpu.make_async_remote_copy(
            src_ref=q_ref.at[k], dst_ref=qbuf.at[k, me],
            send_sem=q_s.at[k, r], recv_sem=q_r.at[k, r],
            device_id={"blk": lax.rem(me + r, nb)}, device_id_type=MESH,
        )

    def q_arrival(k, r):
        return pltpu.make_async_remote_copy(
            src_ref=q_ref.at[k], dst_ref=qbuf.at[k, lax.rem(me + nb - r, nb)],
            send_sem=q_s.at[k, r], recv_sem=q_r.at[k, r],
            device_id={"blk": lax.rem(me + r, nb)}, device_id_type=MESH,
        )

    def p_copy(k, r):
        dst = lax.rem(me + r, nb)
        return pltpu.make_async_remote_copy(
            src_ref=psend.at[k, dst], dst_ref=prec.at[k, me],
            send_sem=p_s.at[k, r], recv_sem=p_r.at[k, r],
            device_id={"blk": dst}, device_id_type=MESH,
        )

    def p_arrival(k, r):
        return pltpu.make_async_remote_copy(
            src_ref=psend.at[k, lax.rem(me + r, nb)],
            dst_ref=prec.at[k, lax.rem(me + nb - r, nb)],
            send_sem=p_s.at[k, r], recv_sem=p_r.at[k, r],
            device_id={"blk": lax.rem(me + r, nb)}, device_id_type=MESH,
        )

    def each_peer(action):
        def step(r, carry):
            action(r)
            return carry
        lax.fori_loop(1, nb, step, 0)

    def send_queries(k, carry):
        each_peer(lambda r: q_copy(k, r).start())
        return carry

    lax.fori_loop(0, kv, send_queries, 0)

    loads[0].wait()
    loads[1].wait()
    owner = lax.broadcasted_iota(jnp.int32, (rows, slots), 0) // groups
    live = lax.broadcasted_iota(jnp.int32, (rows, slots), 1) < len_ref[:, :1]

    def own_head(k, carry):
        q = q_ref[k]
        s = jnp.zeros((rows, slots), F32)
        for i in range(n):
            part = lax.dot_general(q, sk[i, :, head_lanes(k)], NT, preferred_element_type=F32)
            s = jnp.where(owner == i, part, s)
        s = jnp.where(live, s * SCALE, -jnp.inf)
        own = jnp.sum(q.astype(F32) * nk_ref[k].astype(F32), axis=1, keepdims=True) * SCALE
        top = jnp.maximum(jnp.max(s, axis=1, keepdims=True), own)
        wf = jnp.exp(s - top).astype(BF16).astype(F32)
        own_w = jnp.exp(own - top).astype(BF16).astype(F32)
        acc = own_w * nv_ref[k].astype(F32)
        for i in range(n):
            part = jnp.where(owner == i, wf, 0.0).astype(BF16)
            acc += jnp.dot(part, sv[i, :, head_lanes(k)], preferred_element_type=F32)
        lacc[k] = acc
        lm[k] = jnp.broadcast_to(top, (rows, HD))
        lmass[k] = jnp.broadcast_to(jnp.sum(wf, axis=1, keepdims=True) + own_w, (rows, HD))
        return carry

    lax.fori_loop(0, kv, own_head, 0)

    loads[2].wait()
    loads[3].wait()
    stat[...] = jnp.zeros_like(stat)
    chunks = prefix // KEY_CHUNK
    lane = lax.broadcasted_iota(jnp.int32, (nb * rows, HD), 1)

    def prefix_head(k, carry):
        each_peer(lambda r: q_arrival(k, r).wait_recv())
        q = qbuf[k].reshape(nb * rows, HD)
        fold = None
        for c in range(chunks):
            s = lax.dot_general(
                q, pk[pl.ds(c * KEY_CHUNK, KEY_CHUNK), head_lanes(k)], NT,
                preferred_element_type=F32,
            )
            sbuf[:, pl.ds(c * KEY_CHUNK, KEY_CHUNK)] = s
            for p in range(KEY_CHUNK // HD):
                piece = s[:, p * HD:(p + 1) * HD]
                fold = piece if fold is None else jnp.maximum(fold, piece)
        top = (jnp.max(fold, axis=1, keepdims=True) * SCALE).astype(BF16).astype(F32)
        acc = jnp.zeros((nb * rows, HD), F32)
        total = jnp.zeros((nb * rows, HD), F32)
        for c in range(chunks):
            s = sbuf[:, pl.ds(c * KEY_CHUNK, KEY_CHUNK)]
            wb = jnp.exp(s * SCALE - top).astype(BF16)
            acc += jnp.dot(
                wb, pv[pl.ds(c * KEY_CHUNK, KEY_CHUNK), head_lanes(k)],
                preferred_element_type=F32,
            )
            wf = wb.astype(F32)
            for p in range(KEY_CHUNK // HD):
                total += wf[:, p * HD:(p + 1) * HD]
        mass = jnp.sum(total, axis=1, keepdims=True)
        high = mass.astype(BF16).astype(F32)
        psend[k] = acc.astype(BF16).reshape(nb, rows, HD)
        stat[...] = jnp.where(
            lane == k, top,
            jnp.where(lane == kv + k, high, jnp.where(lane == 2 * kv + k, mass - high, stat[...])),
        )
        each_peer(lambda r: p_copy(k, r).start())
        return carry

    lax.fori_loop(0, kv, prefix_head, 0)
    psend[kv] = stat[...].astype(BF16).reshape(nb, rows, HD)
    each_peer(lambda r: p_copy(kv, r).start())
    prec[:, me] = psend[:, me]

    def finish_copies(k, carry):
        each_peer(lambda r: p_arrival(k, r).wait_recv())
        return carry

    lax.fori_loop(0, kv + 1, finish_copies, 0)

    stats = [prec[kv, j].astype(F32) for j in range(nb)]
    for k in range(kv):
        top = lm[k]
        tops = [jnp.broadcast_to(st[:, k:k + 1], (rows, HD)) for st in stats]
        for t in tops:
            top = jnp.maximum(top, t)
        scale = jnp.exp(lm[k] - top)
        acc = lacc[k] * scale
        mass = lmass[k] * scale
        for j in range(nb):
            st = stats[j]
            scale = jnp.exp(tops[j] - top)
            block_mass = st[:, kv + k:kv + k + 1] + st[:, 2 * kv + k:2 * kv + k + 1]
            acc += prec[k, j].astype(F32) * scale
            mass += block_mass * scale
        abuf[mb, k] = (acc / mass).astype(BF16)

    def a_copy(r, slot):
        return pltpu.make_async_remote_copy(
            src_ref=abuf.at[mb], dst_ref=abuf.at[slot],
            send_sem=a_s.at[r], recv_sem=a_r.at[r],
            device_id={"batch": lax.rem(mb + r, nbt)}, device_id_type=MESH,
        )

    for r in range(1, nbt):
        a_copy(r, mb).start()
    for r in range(1, nbt):
        a_copy(r, lax.rem(mb + nbt - r, nbt)).wait_recv()

    for b in range(nbt):
        for k in range(kv):
            a32[b, k] = abuf[b, k].astype(F32)
            for g in range(groups):
                x[b * n:(b + 1) * n, (k * groups + g) * HD:(k * groups + g + 1) * HD] = a32[
                    b, k, pl.ds(g, n, stride=groups), :
                ]
    loads[4].wait()
    xb = x[...].astype(BF16)
    part_rows = osend.shape[1]

    def project(c, carry):
        cols = pl.ds(pl.multiple_of(c * COL_CHUNK, COL_CHUNK), COL_CHUNK)
        part = jnp.dot(xb, w[:, cols], preferred_element_type=F32)
        for t in range(nt):
            osend[t, :, cols] = part[t * part_rows:(t + 1) * part_rows]
        return carry

    lax.fori_loop(0, w.shape[1] // COL_CHUNK, project, 0)

    def o_copy(r, slot):
        dst = lax.rem(mt + r, nt)
        return pltpu.make_async_remote_copy(
            src_ref=osend.at[dst], dst_ref=orecv.at[slot],
            send_sem=o_s.at[r], recv_sem=o_r.at[r],
            device_id={"tensor": dst}, device_id_type=MESH,
        )

    for r in range(1, nt):
        o_copy(r, mt).start()
    result = osend[mt]
    for r in range(1, nt):
        slot = lax.rem(mt + nt - r, nt)
        o_copy(r, slot).wait_recv()
        result = result + orecv[slot]
    o_ref[...] = result.astype(o_ref.dtype)

    def finish_queries(k, carry):
        each_peer(lambda r: q_copy(k, r).wait_send())
        return carry

    def finish_sums(k, carry):
        each_peer(lambda r: p_copy(k, r).wait_send())
        return carry

    lax.fori_loop(0, kv, finish_queries, 0)
    lax.fori_loop(0, kv + 1, finish_sums, 0)
    for r in range(1, nbt):
        a_copy(r, mb).wait_send()
    for r in range(1, nt):
        o_copy(r, mt).wait_send()


def body(
    nb, nbt, nt,
    queries, new_keys, new_values, suffix_keys, suffix_values, suffix_lengths,
    prefix_keys, prefix_values, out_weight,
):
    n = queries.shape[0]
    kv = new_keys.shape[-1] // HD
    groups = queries.shape[-1] // new_keys.shape[-1]
    rows = n * groups
    slots = suffix_keys.shape[1]
    cols = out_weight.shape[1]
    prefix = prefix_keys.shape[0]
    part_rows = nbt * n // nt
    q = queries.reshape(n, kv, groups, HD).transpose(1, 0, 2, 3).reshape(kv, rows, HD)

    def spread(a):
        wide = jnp.broadcast_to(a.reshape(n, kv, HD).transpose(1, 0, 2)[:, :, None], (kv, n, groups, HD))
        return wide.reshape(kv, rows, HD)

    lengths = jnp.broadcast_to(suffix_lengths[:, None, None], (n, groups, HD)).reshape(rows, HD)
    vmem = pl.BlockSpec(memory_space=pltpu.VMEM)
    hbm = pl.BlockSpec(memory_space=pl.ANY)
    dma = pltpu.SemaphoreType.DMA
    flops = 4 * nb * rows * prefix * HD * kv + 2 * nbt * n * out_weight.size
    return pl.pallas_call(
        functools.partial(kernel, nb, nbt, nt, n),
        out_shape=jax.ShapeDtypeStruct((part_rows, cols), BF16),
        in_specs=[vmem] * 4 + [hbm] * 5,
        out_specs=vmem,
        scratch_shapes=[
            pltpu.VMEM(suffix_keys.shape, BF16),
            pltpu.VMEM(suffix_values.shape, BF16),
            pltpu.VMEM(prefix_keys.shape, BF16),
            pltpu.VMEM(prefix_values.shape, BF16),
            pltpu.VMEM(out_weight.shape, BF16),
            pltpu.VMEM((kv, nb, rows, HD), BF16),
            pltpu.VMEM((nb * rows, prefix), F32),
            pltpu.VMEM((nb * rows, HD), F32),
            pltpu.VMEM((kv + 1, nb, rows, HD), BF16),
            pltpu.VMEM((kv + 1, nb, rows, HD), BF16),
            pltpu.VMEM((kv, rows, HD), F32),
            pltpu.VMEM((kv, rows, HD), F32),
            pltpu.VMEM((kv, rows, HD), F32),
            pltpu.VMEM((nbt, kv, rows, HD), BF16),
            pltpu.VMEM((nbt, kv, rows, HD), F32),
            pltpu.VMEM((nbt * n, out_weight.shape[0]), F32),
            pltpu.VMEM((nt, part_rows, cols), F32),
            pltpu.VMEM((nt, part_rows, cols), F32),
            dma((5,)),
            dma((kv, nb)), dma((kv, nb)),
            dma((kv + 1, nb)), dma((kv + 1, nb)),
            dma((nbt,)), dma((nbt,)),
            dma((nt,)), dma((nt,)),
        ],
        compiler_params=pltpu.CompilerParams(
            collective_id=0, has_side_effects=True, vmem_limit_bytes=56 * 2**20
        ),
        cost_estimate=pl.CostEstimate(
            flops=flops,
            bytes_accessed=2 * (2 * suffix_keys.size + 2 * prefix_keys.size + out_weight.size),
            transcendentals=kv * rows * (nb * prefix + slots),
        ),
    )(q, spread(new_keys), spread(new_values), lengths, suffix_keys, suffix_values,
      prefix_keys, prefix_values, out_weight)


def solution(mesh):
    in_specs = (
        P(("blk", "batch"), "tensor"),
        P(("blk", "batch"), "tensor"),
        P(("blk", "batch"), "tensor"),
        P(("blk", "batch"), None, "tensor"),
        P(("blk", "batch"), None, "tensor"),
        P(("blk", "batch")),
        P("blk", "tensor"),
        P("blk", "tensor"),
        P("tensor", "batch"),
    )
    out_specs = P(("blk", "tensor"), "batch")
    sizes = (mesh.shape["blk"], mesh.shape["batch"], mesh.shape["tensor"])
    return jax.shard_map(
        functools.partial(body, *sizes), mesh=mesh, in_specs=in_specs, out_specs=out_specs,
        check_vma=False,
    )
```

```python
import functools

import jax
import jax.numpy as jnp
from jax import lax
from jax.experimental import pallas as pl
from jax.experimental.pallas import tpu as pltpu
from jax.sharding import PartitionSpec as P

HD = 128
SCALE = HD ** (-0.5)
F32 = jnp.float32
BF16 = jnp.bfloat16
MESH = pl.DeviceIdType.MESH
NT = (((1,), (1,)), ((), ()))
KEY_CHUNK = 512
COL_CHUNK = 256


def head_lanes(k):
    return pl.ds(pl.multiple_of(k * HD, HD), HD)


def kernel(
    nb, nbt, nt, n,
    q_ref, nk_ref, nv_ref, len_ref, sk_hbm, sv_hbm, pk_hbm, pv_hbm, w_hbm,
    o_ref,
    sk, sv, pk, pv, w, q32, nk32, nv32, qsrc, qbuf, sbuf, stat, psend, prec, lacc, lm, lmass,
    abuf, a32, x, osend, orecv,
    lsem, k_s, k_r, q_s, q_r, p_s, p_r, a_s, a_r, o_s, o_r,
):
    kv, rows, _ = q32.shape
    groups = rows // n
    half = kv // 2
    slots = sk.shape[1]
    prefix = pk.shape[1]
    me = lax.axis_index("blk")
    mb = lax.axis_index("batch")
    mt = lax.axis_index("tensor")
    core = lax.rem(me, 2)
    pair = me + 1 - 2 * core

    def half_lanes(c):
        return pl.ds(pl.multiple_of(c * half * HD, half * HD), half * HD)

    barrier = pltpu.get_barrier_semaphore()
    for axis, mine, size in (("blk", me, nb), ("batch", mb, nbt), ("tensor", mt, nt)):
        for r in range(1, size):
            pl.semaphore_signal(
                barrier, inc=1, device_id={axis: lax.rem(mine + r, size)}, device_id_type=MESH
            )
    loads = [
        pltpu.make_async_copy(src, dst, lsem.at[i])
        for i, (src, dst) in enumerate([
            (sk_hbm, sk), (sv_hbm, sv), (pk_hbm.at[:, half_lanes(core)], pk.at[0]),
            (pv_hbm.at[:, half_lanes(core)], pv.at[0]), (w_hbm, w),
        ])
    ]
    for load in loads[:4]:
        load.start()

    qf = q_ref[...].astype(F32)
    for k in range(kv):
        for g in range(groups):
            h = k * groups + g
            q32[k, pl.ds(g, n, stride=groups), :] = qf[:, h * HD:(h + 1) * HD]
        qsrc[k] = q32[k].astype(BF16)
    qbuf[me] = qsrc[pl.ds(core * half, half)]
    pl.semaphore_wait(barrier, nb + nbt + nt - 3)

    def q_copy(r, slot):
        dst = lax.rem(me + r, nb)
        return pltpu.make_async_remote_copy(
            src_ref=qsrc.at[pl.ds(lax.rem(dst, 2) * half, half)], dst_ref=qbuf.at[slot],
            send_sem=q_s.at[r], recv_sem=q_r.at[r],
            device_id={"blk": dst}, device_id_type=MESH,
        )

    def pair_copy(i, src, dst):
        return pltpu.make_async_remote_copy(
            src_ref=src.at[:, half_lanes(1 - core)], dst_ref=dst.at[1],
            send_sem=k_s.at[i], recv_sem=k_r.at[i],
            device_id={"blk": pair}, device_id_type=MESH,
        )

    def p_copy(part, r, slot):
        dst = lax.rem(me + r, nb)
        span = pl.ds(0, half - 1) if part == 0 else pl.ds(half - 1, 2)
        return pltpu.make_async_remote_copy(
            src_ref=psend.at[dst, span], dst_ref=prec.at[slot, span],
            send_sem=p_s.at[part, r], recv_sem=p_r.at[part, r],
            device_id={"blk": dst}, device_id_type=MESH,
        )

    def source(r):
        return lax.rem(me + nb - r, nb)

    def each_peer(action):
        def step(r, carry):
            action(r)
            return carry
        lax.fori_loop(1, nb, step, 0)

    each_peer(lambda r: q_copy(r, me).start())
    swaps = [pair_copy(0, pk_hbm, pk), pair_copy(1, pv_hbm, pv)]
    for swap in swaps:
        swap.start()
    loads[4].start()

    nkf, nvf = nk_ref[...].astype(F32), nv_ref[...].astype(F32)
    for k in range(kv):
        for i in range(n):
            span = slice(i * groups, (i + 1) * groups)
            nk32[k, span, :] = jnp.broadcast_to(nkf[i:i + 1, k * HD:(k + 1) * HD], (groups, HD))
            nv32[k, span, :] = jnp.broadcast_to(nvf[i:i + 1, k * HD:(k + 1) * HD], (groups, HD))

    loads[0].wait()
    loads[1].wait()
    owner = lax.broadcasted_iota(jnp.int32, (rows, slots), 0) // groups
    lengths = jnp.zeros((rows, slots), jnp.int32)
    for i in range(n):
        lengths = jnp.where(owner == i, len_ref[i], lengths)
    live = lax.broadcasted_iota(jnp.int32, (rows, slots), 1) < lengths

    def own_head(k, carry):
        q = qsrc[k]
        s = jnp.zeros((rows, slots), F32)
        for i in range(n):
            part = lax.dot_general(q, sk[i, :, head_lanes(k)], NT, preferred_element_type=F32)
            s = jnp.where(owner == i, part, s)
        s = jnp.where(live, s * SCALE, -jnp.inf)
        own = jnp.sum(q32[k] * nk32[k], axis=1, keepdims=True) * SCALE
        top = jnp.maximum(jnp.max(s, axis=1, keepdims=True), own)
        wf = jnp.exp(s - top).astype(BF16).astype(F32)
        own_w = jnp.exp(own - top).astype(BF16).astype(F32)
        acc = own_w * nv32[k]
        for i in range(n):
            part = jnp.where(owner == i, wf, 0.0).astype(BF16)
            acc += jnp.dot(part, sv[i, :, head_lanes(k)], preferred_element_type=F32)
        lacc[k] = acc
        lm[k] = jnp.broadcast_to(top, (rows, HD))
        lmass[k] = jnp.broadcast_to(jnp.sum(wf, axis=1, keepdims=True) + own_w, (rows, HD))
        return carry

    lax.fori_loop(0, kv, own_head, 0)

    loads[2].wait()
    loads[3].wait()
    for swap in swaps:
        swap.wait_recv()
    each_peer(lambda r: q_copy(r, source(r)).wait_recv())
    chunks = [
        (b, pl.ds(c * KEY_CHUNK, KEY_CHUNK), pl.ds(b * prefix + c * KEY_CHUNK, KEY_CHUNK))
        for b in range(2) for c in range(prefix // KEY_CHUNK)
    ]
    lane = lax.broadcasted_iota(jnp.int32, (nb * rows, HD), 1)
    stat[...] = jnp.zeros_like(stat)

    def prefix_head(k):
        lanes = pl.ds(k * HD, HD)
        q = qbuf[:, k].reshape(nb * rows, HD)
        fold = None
        for b, span, place in chunks:
            s = lax.dot_general(q, pk[b, span, lanes], NT, preferred_element_type=F32)
            sbuf[:, place] = s
            for p in range(KEY_CHUNK // HD):
                piece = s[:, p * HD:(p + 1) * HD]
                fold = piece if fold is None else jnp.maximum(fold, piece)
        top = (jnp.max(fold, axis=1, keepdims=True) * SCALE).astype(BF16).astype(F32)
        acc = jnp.zeros((nb * rows, HD), F32)
        total = jnp.zeros((nb * rows, HD), F32)
        for b, span, place in chunks:
            wb = jnp.exp(sbuf[:, place] * SCALE - top).astype(BF16)
            acc += jnp.dot(wb, pv[b, span, lanes], preferred_element_type=F32)
            wf = wb.astype(F32)
            for p in range(KEY_CHUNK // HD):
                total += wf[:, p * HD:(p + 1) * HD]
        mass = jnp.sum(total, axis=1, keepdims=True)
        high = mass.astype(BF16).astype(F32)
        psend[:, k] = acc.astype(BF16).reshape(nb, rows, HD)
        stat[...] = jnp.where(
            lane == k, top,
            jnp.where(
                lane == half + k, high, jnp.where(lane == 2 * half + k, mass - high, stat[...])
            ),
        )

    for k in range(half):
        prefix_head(k)
        if k == half - 2:
            each_peer(lambda r: p_copy(0, r, me).start())
    psend[:, half] = stat[...].astype(BF16).reshape(nb, rows, HD)
    each_peer(lambda r: p_copy(1, r, me).start())
    prec[me] = psend[me]
    each_peer(lambda r: p_copy(0, r, source(r)).wait_recv())
    each_peer(lambda r: p_copy(1, r, source(r)).wait_recv())

    stats = [prec[j, half].astype(F32) for j in range(nb)]
    for h in range(kv):
        k = h % half
        sources = range(h // half, nb, 2)
        top = lm[h]
        tops = {j: jnp.broadcast_to(stats[j][:, k:k + 1], (rows, HD)) for j in sources}
        for j in sources:
            top = jnp.maximum(top, tops[j])
        scale = jnp.exp(lm[h] - top)
        acc = lacc[h] * scale
        mass = lmass[h] * scale
        for j in sources:
            st = stats[j]
            scale = jnp.exp(tops[j] - top)
            acc += prec[j, k].astype(F32) * scale
            mass += scale * (
                st[:, half + k:half + k + 1] + st[:, 2 * half + k:2 * half + k + 1]
            )
        abuf[mb, h] = (acc / mass).astype(BF16)

    def a_copy(r, slot):
        return pltpu.make_async_remote_copy(
            src_ref=abuf.at[mb], dst_ref=abuf.at[slot],
            send_sem=a_s.at[r], recv_sem=a_r.at[r],
            device_id={"batch": lax.rem(mb + r, nbt)}, device_id_type=MESH,
        )

    for r in range(1, nbt):
        a_copy(r, mb).start()
    for r in range(1, nbt):
        a_copy(r, lax.rem(mb + nbt - r, nbt)).wait_recv()

    for b in range(nbt):
        for k in range(kv):
            a32[b, k] = abuf[b, k].astype(F32)
            for g in range(groups):
                x[b * n:(b + 1) * n, (k * groups + g) * HD:(k * groups + g + 1) * HD] = a32[
                    b, k, pl.ds(g, n, stride=groups), :
                ]
    loads[4].wait()
    xb = x[...].astype(BF16)
    part_rows = osend.shape[1]

    def project(c, carry):
        cols = pl.ds(pl.multiple_of(c * COL_CHUNK, COL_CHUNK), COL_CHUNK)
        part = jnp.dot(xb, w[:, cols], preferred_element_type=F32)
        for t in range(nt):
            osend[t, :, cols] = part[t * part_rows:(t + 1) * part_rows]
        return carry

    lax.fori_loop(0, w.shape[1] // COL_CHUNK, project, 0)

    def o_copy(r, slot):
        dst = lax.rem(mt + r, nt)
        return pltpu.make_async_remote_copy(
            src_ref=osend.at[dst], dst_ref=orecv.at[slot],
            send_sem=o_s.at[r], recv_sem=o_r.at[r],
            device_id={"tensor": dst}, device_id_type=MESH,
        )

    for r in range(1, nt):
        o_copy(r, mt).start()
    result = osend[mt]
    for r in range(1, nt):
        slot = lax.rem(mt + nt - r, nt)
        o_copy(r, slot).wait_recv()
        result = result + orecv[slot]
    o_ref[...] = result

    each_peer(lambda r: q_copy(r, me).wait_send())
    each_peer(lambda r: p_copy(0, r, me).wait_send())
    each_peer(lambda r: p_copy(1, r, me).wait_send())
    for swap in swaps:
        swap.wait_send()
    for r in range(1, nbt):
        a_copy(r, mb).wait_send()
    for r in range(1, nt):
        o_copy(r, mt).wait_send()


def body(
    nb, nbt, nt,
    queries, new_keys, new_values, suffix_keys, suffix_values, suffix_lengths,
    prefix_keys, prefix_values, out_weight,
):
    n = queries.shape[0]
    kv = new_keys.shape[-1] // HD
    groups = queries.shape[-1] // new_keys.shape[-1]
    rows = n * groups
    slots = suffix_keys.shape[1]
    cols = out_weight.shape[1]
    prefix = prefix_keys.shape[0]
    part_rows = nbt * n // nt
    half = kv // 2
    vmem = pl.BlockSpec(memory_space=pltpu.VMEM)
    smem = pl.BlockSpec(memory_space=pltpu.SMEM)
    hbm = pl.BlockSpec(memory_space=pl.ANY)
    dma = pltpu.SemaphoreType.DMA
    flops = 4 * nb * rows * prefix * HD * kv + 2 * nbt * n * out_weight.size
    return pl.pallas_call(
        functools.partial(kernel, nb, nbt, nt, n),
        out_shape=jax.ShapeDtypeStruct((part_rows, cols), F32),
        in_specs=[vmem] * 3 + [smem] + [hbm] * 5,
        out_specs=vmem,
        scratch_shapes=[
            pltpu.VMEM(suffix_keys.shape, BF16),
            pltpu.VMEM(suffix_values.shape, BF16),
            pltpu.VMEM((2, prefix, half * HD), BF16),
            pltpu.VMEM((2, prefix, half * HD), BF16),
            pltpu.VMEM(out_weight.shape, BF16),
            pltpu.VMEM((kv, rows, HD), F32),
            pltpu.VMEM((kv, rows, HD), F32),
            pltpu.VMEM((kv, rows, HD), F32),
            pltpu.VMEM((kv, rows, HD), BF16),
            pltpu.VMEM((nb, half, rows, HD), BF16),
            pltpu.VMEM((nb * rows, 2 * prefix), F32),
            pltpu.VMEM((nb * rows, HD), F32),
            pltpu.VMEM((nb, half + 1, rows, HD), BF16),
            pltpu.VMEM((nb, half + 1, rows, HD), BF16),
            pltpu.VMEM((kv, rows, HD), F32),
            pltpu.VMEM((kv, rows, HD), F32),
            pltpu.VMEM((kv, rows, HD), F32),
            pltpu.VMEM((nbt, kv, rows, HD), BF16),
            pltpu.VMEM((nbt, kv, rows, HD), F32),
            pltpu.VMEM((nbt * n, out_weight.shape[0]), F32),
            pltpu.VMEM((nt, part_rows, cols), F32),
            pltpu.VMEM((nt, part_rows, cols), F32),
            dma((5,)),
            dma((2,)), dma((2,)),
            dma((nb,)), dma((nb,)),
            dma((2, nb)), dma((2, nb)),
            dma((nbt,)), dma((nbt,)),
            dma((nt,)), dma((nt,)),
        ],
        compiler_params=pltpu.CompilerParams(
            collective_id=0, has_side_effects=True, vmem_limit_bytes=56 * 2**20
        ),
        cost_estimate=pl.CostEstimate(
            flops=flops,
            bytes_accessed=2 * (2 * suffix_keys.size + 2 * prefix_keys.size + out_weight.size),
            transcendentals=kv * rows * (nb * prefix + slots),
        ),
    )(queries, new_keys, new_values, suffix_lengths, suffix_keys, suffix_values,
      prefix_keys, prefix_values, out_weight).astype(BF16)


def solution(mesh):
    in_specs = (
        P(("blk", "batch"), "tensor"),
        P(("blk", "batch"), "tensor"),
        P(("blk", "batch"), "tensor"),
        P(("blk", "batch"), None, "tensor"),
        P(("blk", "batch"), None, "tensor"),
        P(("blk", "batch")),
        P("blk", "tensor"),
        P("blk", "tensor"),
        P("tensor", "batch"),
    )
    out_specs = P(("blk", "tensor"), "batch")
    sizes = (mesh.shape["blk"], mesh.shape["batch"], mesh.shape["tensor"])
    return jax.shard_map(
        functools.partial(body, *sizes), mesh=mesh, in_specs=in_specs, out_specs=out_specs,
        check_vma=False,
    )
```

```python
import functools

import jax
import jax.numpy as jnp
from jax import lax
from jax.experimental import pallas as pl
from jax.experimental.pallas import tpu as pltpu
from jax.sharding import PartitionSpec as P

HD = 128
SCALE = HD ** (-0.5)
F32 = jnp.float32
BF16 = jnp.bfloat16
MESH = pl.DeviceIdType.MESH
NT = (((1,), (1,)), ((), ()))
KEY_CHUNK = 512
COL_CHUNK = 256


def head_lanes(k):
    return pl.ds(pl.multiple_of(k * HD, HD), HD)


def kernel(
    nb, nbt, nt, n,
    q_ref, nk_ref, nv_ref, len_ref, sk_hbm, sv_hbm, pk_hbm, pv_hbm, w_hbm,
    o_ref,
    sk, sv, pk, pv, w, q32, nk32, nv32, qsrc, qbuf, sbuf, psend, prec, lacc, lm, lmass,
    abuf, a32, x, osend, orecv,
    lsem, k_s, k_r, q_s, q_r, p_s, p_r, a_s, a_r, o_s, o_r,
):
    kv, rows, _ = q32.shape
    groups = rows // n
    half = kv // 2
    slots = sk.shape[1]
    prefix = pk.shape[1]
    me = lax.axis_index("blk")
    mb = lax.axis_index("batch")
    mt = lax.axis_index("tensor")
    core = lax.rem(me, 2)
    pair = me + 1 - 2 * core

    def half_lanes(c):
        return pl.ds(pl.multiple_of(c * half * HD, half * HD), half * HD)

    barrier = pltpu.get_barrier_semaphore()
    for axis, mine, size in (("blk", me, nb), ("batch", mb, nbt), ("tensor", mt, nt)):
        for r in range(1, size):
            pl.semaphore_signal(
                barrier, inc=1, device_id={axis: lax.rem(mine + r, size)}, device_id_type=MESH
            )
    loads = [
        pltpu.make_async_copy(src, dst, lsem.at[i])
        for i, (src, dst) in enumerate([
            (sk_hbm, sk), (sv_hbm, sv), (pk_hbm.at[:, half_lanes(core)], pk.at[0]),
            (pv_hbm.at[:, half_lanes(core)], pv.at[0]), (w_hbm, w),
        ])
    ]
    for load in loads:
        load.start()

    qf = q_ref[...].astype(F32)
    for k in range(kv):
        for g in range(groups):
            h = k * groups + g
            q32[k, pl.ds(g, n, stride=groups), :] = qf[:, h * HD:(h + 1) * HD]
        qsrc[k] = q32[k].astype(BF16)
    qbuf[me] = qsrc[pl.ds(core * half, half)]
    pl.semaphore_wait(barrier, nb + nbt + nt - 3)

    def q_copy(r, slot):
        dst = lax.rem(me + r, nb)
        return pltpu.make_async_remote_copy(
            src_ref=qsrc.at[pl.ds(lax.rem(dst, 2) * half, half)], dst_ref=qbuf.at[slot],
            send_sem=q_s.at[r], recv_sem=q_r.at[r],
            device_id={"blk": dst}, device_id_type=MESH,
        )

    def pair_copy(i, src, dst):
        return pltpu.make_async_remote_copy(
            src_ref=src.at[:, half_lanes(1 - core)], dst_ref=dst.at[1],
            send_sem=k_s.at[i], recv_sem=k_r.at[i],
            device_id={"blk": pair}, device_id_type=MESH,
        )

    def p_copy(k, r, slot):
        dst = lax.rem(me + r, nb)
        return pltpu.make_async_remote_copy(
            src_ref=psend.at[k, dst], dst_ref=prec.at[k, slot],
            send_sem=p_s.at[k, r], recv_sem=p_r.at[k, r],
            device_id={"blk": dst}, device_id_type=MESH,
        )

    def source(r):
        return lax.rem(me + nb - r, nb)

    def each_peer(action):
        def step(r, carry):
            action(r)
            return carry
        lax.fori_loop(1, nb, step, 0)

    each_peer(lambda r: q_copy(r, me).start())
    swaps = [pair_copy(0, pk_hbm, pk), pair_copy(1, pv_hbm, pv)]
    for swap in swaps:
        swap.start()

    nkf, nvf = nk_ref[...].astype(F32), nv_ref[...].astype(F32)
    for k in range(kv):
        for i in range(n):
            span = slice(i * groups, (i + 1) * groups)
            nk32[k, span, :] = jnp.broadcast_to(nkf[i:i + 1, k * HD:(k + 1) * HD], (groups, HD))
            nv32[k, span, :] = jnp.broadcast_to(nvf[i:i + 1, k * HD:(k + 1) * HD], (groups, HD))

    loads[0].wait()
    loads[1].wait()
    owner = lax.broadcasted_iota(jnp.int32, (rows, slots), 0) // groups
    lengths = jnp.zeros((rows, slots), jnp.int32)
    for i in range(n):
        lengths = jnp.where(owner == i, len_ref[i], lengths)
    live = lax.broadcasted_iota(jnp.int32, (rows, slots), 1) < lengths

    def own_head(k, carry):
        q = qsrc[k]
        s = jnp.zeros((rows, slots), F32)
        for i in range(n):
            part = lax.dot_general(q, sk[i, :, head_lanes(k)], NT, preferred_element_type=F32)
            s = jnp.where(owner == i, part, s)
        s = jnp.where(live, s * SCALE, -jnp.inf)
        own = jnp.sum(q32[k] * nk32[k], axis=1, keepdims=True) * SCALE
        top = jnp.maximum(jnp.max(s, axis=1, keepdims=True), own)
        wf = jnp.exp(s - top).astype(BF16).astype(F32)
        own_w = jnp.exp(own - top).astype(BF16).astype(F32)
        acc = own_w * nv32[k]
        for i in range(n):
            part = jnp.where(owner == i, wf, 0.0).astype(BF16)
            acc += jnp.dot(part, sv[i, :, head_lanes(k)], preferred_element_type=F32)
        lacc[k] = acc
        lm[k] = jnp.broadcast_to(top, (rows, HD))
        lmass[k] = jnp.broadcast_to(jnp.sum(wf, axis=1, keepdims=True) + own_w, (rows, HD))
        return carry

    lax.fori_loop(0, kv, own_head, 0)

    loads[2].wait()
    loads[3].wait()
    for swap in swaps:
        swap.wait_recv()
    each_peer(lambda r: q_copy(r, source(r)).wait_recv())
    chunks = [
        (b, pl.ds(c * KEY_CHUNK, KEY_CHUNK), pl.ds(b * prefix + c * KEY_CHUNK, KEY_CHUNK))
        for b in range(2) for c in range(prefix // KEY_CHUNK)
    ]
    lane = lax.broadcasted_iota(jnp.int32, (nb * rows, HD), 1)

    def prefix_head(k):
        lanes = pl.ds(k * HD, HD)
        q = qbuf[:, k].reshape(nb * rows, HD)
        fold = None
        for b, span, place in chunks:
            s = lax.dot_general(q, pk[b, span, lanes], NT, preferred_element_type=F32)
            sbuf[:, place] = s
            for p in range(KEY_CHUNK // HD):
                piece = s[:, p * HD:(p + 1) * HD]
                fold = piece if fold is None else jnp.maximum(fold, piece)
        top = (jnp.max(fold, axis=1, keepdims=True) * SCALE).astype(BF16).astype(F32)
        acc = jnp.zeros((nb * rows, HD), F32)
        total = jnp.zeros((nb * rows, HD), F32)
        for b, span, place in chunks:
            wb = jnp.exp(sbuf[:, place] * SCALE - top).astype(BF16)
            acc += jnp.dot(wb, pv[b, span, lanes], preferred_element_type=F32)
            wf = wb.astype(F32)
            for p in range(KEY_CHUNK // HD):
                total += wf[:, p * HD:(p + 1) * HD]
        mass = jnp.sum(total, axis=1, keepdims=True)
        high = mass.astype(BF16).astype(F32)
        stat = jnp.where(lane == 0, top, jnp.where(lane == 1, high, mass - high))
        psend[k, :, 0] = acc.astype(BF16).reshape(nb, rows, HD)
        psend[k, :, 1] = stat.astype(BF16).reshape(nb, rows, HD)

    for k in range(half):
        prefix_head(k)
        each_peer(functools.partial(lambda k, r: p_copy(k, r, me).start(), k))
        prec[k, me] = psend[k, me]

    def join(k):
        for p in range(2):
            h = p * half + k
            sources = range(p, nb, 2)
            stats = {j: prec[k, j, 1].astype(F32) for j in sources}
            tops = {j: jnp.broadcast_to(stats[j][:, :1], (rows, HD)) for j in sources}
            top = lm[h]
            for j in sources:
                top = jnp.maximum(top, tops[j])
            scale = jnp.exp(lm[h] - top)
            acc = lacc[h] * scale
            mass = lmass[h] * scale
            for j in sources:
                scale = jnp.exp(tops[j] - top)
                acc += prec[k, j, 0].astype(F32) * scale
                mass += scale * (stats[j][:, 1:2] + stats[j][:, 2:3])
            abuf[k, mb, p] = (acc / mass).astype(BF16)

    def a_copy(k, r, slot):
        return pltpu.make_async_remote_copy(
            src_ref=abuf.at[k, mb], dst_ref=abuf.at[k, slot],
            send_sem=a_s.at[k, r], recv_sem=a_r.at[k, r],
            device_id={"batch": lax.rem(mb + r, nbt)}, device_id_type=MESH,
        )

    part_rows = osend.shape[1]
    depth = groups * HD

    def project(k):
        for b in range(nbt):
            for p in range(2):
                h = p * half + k
                a32[b, h] = abuf[k, b, p].astype(F32)
                for g in range(groups):
                    x[b * n:(b + 1) * n, h * depth + g * HD:h * depth + (g + 1) * HD] = a32[
                        b, h, pl.ds(g, n, stride=groups), :
                    ]
        spans = [pl.ds((p * half + k) * depth, depth) for p in range(2)]
        xs = [x[:, span].astype(BF16) for span in spans]

        def column_block(c, carry):
            cols = pl.ds(pl.multiple_of(c * COL_CHUNK, COL_CHUNK), COL_CHUNK)
            part = jnp.dot(xs[0], w[spans[0], cols], preferred_element_type=F32)
            part += jnp.dot(xs[1], w[spans[1], cols], preferred_element_type=F32)
            for t in range(nt):
                piece = part[t * part_rows:(t + 1) * part_rows]
                osend[t, :, cols] = piece if k == 0 else osend[t, :, cols] + piece
            return carry

        lax.fori_loop(0, w.shape[1] // COL_CHUNK, column_block, 0)

    for k in range(half):
        each_peer(functools.partial(lambda k, r: p_copy(k, r, source(r)).wait_recv(), k))
        join(k)
        for r in range(1, nbt):
            a_copy(k, r, mb).start()
        for r in range(1, nbt):
            a_copy(k, r, lax.rem(mb + nbt - r, nbt)).wait_recv()
        if k == 0:
            loads[4].wait()
        project(k)

    def o_copy(r, slot):
        dst = lax.rem(mt + r, nt)
        return pltpu.make_async_remote_copy(
            src_ref=osend.at[dst], dst_ref=orecv.at[slot],
            send_sem=o_s.at[r], recv_sem=o_r.at[r],
            device_id={"tensor": dst}, device_id_type=MESH,
        )

    for r in range(1, nt):
        o_copy(r, mt).start()
    result = osend[mt]
    for r in range(1, nt):
        slot = lax.rem(mt + nt - r, nt)
        o_copy(r, slot).wait_recv()
        result = result + orecv[slot]
    o_ref[...] = result

    each_peer(lambda r: q_copy(r, me).wait_send())
    for k in range(half):
        each_peer(functools.partial(lambda k, r: p_copy(k, r, me).wait_send(), k))
        for r in range(1, nbt):
            a_copy(k, r, mb).wait_send()
    for swap in swaps:
        swap.wait_send()
    for r in range(1, nt):
        o_copy(r, mt).wait_send()


def body(
    nb, nbt, nt,
    queries, new_keys, new_values, suffix_keys, suffix_values, suffix_lengths,
    prefix_keys, prefix_values, out_weight,
):
    n = queries.shape[0]
    kv = new_keys.shape[-1] // HD
    groups = queries.shape[-1] // new_keys.shape[-1]
    rows = n * groups
    slots = suffix_keys.shape[1]
    cols = out_weight.shape[1]
    prefix = prefix_keys.shape[0]
    part_rows = nbt * n // nt
    half = kv // 2
    vmem = pl.BlockSpec(memory_space=pltpu.VMEM)
    smem = pl.BlockSpec(memory_space=pltpu.SMEM)
    hbm = pl.BlockSpec(memory_space=pl.ANY)
    dma = pltpu.SemaphoreType.DMA
    flops = 4 * nb * rows * prefix * HD * kv + 2 * nbt * n * out_weight.size
    return pl.pallas_call(
        functools.partial(kernel, nb, nbt, nt, n),
        out_shape=jax.ShapeDtypeStruct((part_rows, cols), F32),
        in_specs=[vmem] * 3 + [smem] + [hbm] * 5,
        out_specs=vmem,
        scratch_shapes=[
            pltpu.VMEM(suffix_keys.shape, BF16),
            pltpu.VMEM(suffix_values.shape, BF16),
            pltpu.VMEM((2, prefix, half * HD), BF16),
            pltpu.VMEM((2, prefix, half * HD), BF16),
            pltpu.VMEM(out_weight.shape, BF16),
            pltpu.VMEM((kv, rows, HD), F32),
            pltpu.VMEM((kv, rows, HD), F32),
            pltpu.VMEM((kv, rows, HD), F32),
            pltpu.VMEM((kv, rows, HD), BF16),
            pltpu.VMEM((nb, half, rows, HD), BF16),
            pltpu.VMEM((nb * rows, 2 * prefix), F32),
            pltpu.VMEM((half, nb, 2, rows, HD), BF16),
            pltpu.VMEM((half, nb, 2, rows, HD), BF16),
            pltpu.VMEM((kv, rows, HD), F32),
            pltpu.VMEM((kv, rows, HD), F32),
            pltpu.VMEM((kv, rows, HD), F32),
            pltpu.VMEM((half, nbt, 2, rows, HD), BF16),
            pltpu.VMEM((nbt, kv, rows, HD), F32),
            pltpu.VMEM((nbt * n, out_weight.shape[0]), F32),
            pltpu.VMEM((nt, part_rows, cols), F32),
            pltpu.VMEM((nt, part_rows, cols), F32),
            dma((5,)),
            dma((2,)), dma((2,)),
            dma((nb,)), dma((nb,)),
            dma((half, nb)), dma((half, nb)),
            dma((half, nbt)), dma((half, nbt)),
            dma((nt,)), dma((nt,)),
        ],
        compiler_params=pltpu.CompilerParams(
            collective_id=0, has_side_effects=True, vmem_limit_bytes=56 * 2**20
        ),
        cost_estimate=pl.CostEstimate(
            flops=flops,
            bytes_accessed=2 * (2 * suffix_keys.size + 2 * prefix_keys.size + out_weight.size),
            transcendentals=kv * rows * (nb * prefix + slots),
        ),
    )(queries, new_keys, new_values, suffix_lengths, suffix_keys, suffix_values,
      prefix_keys, prefix_values, out_weight).astype(BF16)


def solution(mesh):
    in_specs = (
        P(("blk", "batch"), "tensor"),
        P(("blk", "batch"), "tensor"),
        P(("blk", "batch"), "tensor"),
        P(("blk", "batch"), None, "tensor"),
        P(("blk", "batch"), None, "tensor"),
        P(("blk", "batch")),
        P("blk", "tensor"),
        P("blk", "tensor"),
        P("tensor", "batch"),
    )
    out_specs = P(("blk", "tensor"), "batch")
    sizes = (mesh.shape["blk"], mesh.shape["batch"], mesh.shape["tensor"])
    return jax.shard_map(
        functools.partial(body, *sizes), mesh=mesh, in_specs=in_specs, out_specs=out_specs,
        check_vma=False,
    )
```

```python
import functools

import jax
import jax.numpy as jnp
from jax import lax
from jax.experimental import pallas as pl
from jax.experimental.pallas import tpu as pltpu
from jax.sharding import PartitionSpec as P

HD = 128
SCALE = HD ** (-0.5)
F32 = jnp.float32
BF16 = jnp.bfloat16
MESH = pl.DeviceIdType.MESH
NT = (((1,), (1,)), ((), ()))
KEY_CHUNK = 512
COL_CHUNK = 256


def head_lanes(k):
    return pl.ds(pl.multiple_of(k * HD, HD), HD)


def kernel(
    nb, nbt, nt, n,
    q_ref, nk_ref, nv_ref, len_ref, sk_hbm, sv_hbm, pk_hbm, pv_hbm, w_hbm,
    o_ref,
    sk, sv, pk, pv, w, q32, nk32, nv32, qsrc, qbuf, sbuf, psend, prec, lacc, lm, lmass,
    abuf, a32, x, osend, orecv,
    lsem, k_s, k_r, q_s, q_r, p_s, p_r, a_s, a_r, o_s, o_r,
):
    kv, rows, _ = q32.shape
    groups = rows // n
    half = kv // 2
    slots = sk.shape[1]
    prefix = pk.shape[1]
    me = lax.axis_index("blk")
    mb = lax.axis_index("batch")
    mt = lax.axis_index("tensor")
    core = lax.rem(me, 2)
    pair = me + 1 - 2 * core

    def half_lanes(c):
        return pl.ds(pl.multiple_of(c * half * HD, half * HD), half * HD)

    barrier = pltpu.get_barrier_semaphore()
    for axis, mine, size in (("blk", me, nb), ("batch", mb, nbt), ("tensor", mt, nt)):
        for r in range(1, size):
            pl.semaphore_signal(
                barrier, inc=1, device_id={axis: lax.rem(mine + r, size)}, device_id_type=MESH
            )
    loads = [
        pltpu.make_async_copy(src, dst, lsem.at[i])
        for i, (src, dst) in enumerate([
            (sk_hbm, sk), (sv_hbm, sv), (pk_hbm.at[:, half_lanes(core)], pk.at[0]),
            (pv_hbm.at[:, half_lanes(core)], pv.at[0]), (w_hbm, w),
        ])
    ]
    for load in loads:
        load.start()

    qf = q_ref[...].astype(F32)
    for k in range(kv):
        for g in range(groups):
            h = k * groups + g
            q32[k, pl.ds(g, n, stride=groups), :] = qf[:, h * HD:(h + 1) * HD]
        qsrc[k] = q32[k].astype(BF16)
    qbuf[me] = qsrc[pl.ds(core * half, half)]
    pl.semaphore_wait(barrier, nb + nbt + nt - 3)

    def q_copy(r, slot):
        dst = lax.rem(me + r, nb)
        return pltpu.make_async_remote_copy(
            src_ref=qsrc.at[pl.ds(lax.rem(dst, 2) * half, half)], dst_ref=qbuf.at[slot],
            send_sem=q_s.at[r], recv_sem=q_r.at[r],
            device_id={"blk": dst}, device_id_type=MESH,
        )

    def pair_copy(i, src, dst):
        return pltpu.make_async_remote_copy(
            src_ref=src.at[:, half_lanes(1 - core)], dst_ref=dst.at[1],
            send_sem=k_s.at[i], recv_sem=k_r.at[i],
            device_id={"blk": pair}, device_id_type=MESH,
        )

    def p_copy(k, r, slot):
        dst = lax.rem(me + r, nb)
        return pltpu.make_async_remote_copy(
            src_ref=psend.at[k, dst], dst_ref=prec.at[k, slot],
            send_sem=p_s.at[k, r], recv_sem=p_r.at[k, r],
            device_id={"blk": dst}, device_id_type=MESH,
        )

    def source(r):
        return lax.rem(me + nb - r, nb)

    def each_peer(action):
        def step(r, carry):
            action(r)
            return carry
        lax.fori_loop(1, nb, step, 0)

    each_peer(lambda r: q_copy(r, me).start())
    swaps = [pair_copy(0, pk_hbm, pk), pair_copy(1, pv_hbm, pv)]
    for swap in swaps:
        swap.start()

    nkf, nvf = nk_ref[...].astype(F32), nv_ref[...].astype(F32)
    for k in range(kv):
        for i in range(n):
            span = slice(i * groups, (i + 1) * groups)
            nk32[k, span, :] = jnp.broadcast_to(nkf[i:i + 1, k * HD:(k + 1) * HD], (groups, HD))
            nv32[k, span, :] = jnp.broadcast_to(nvf[i:i + 1, k * HD:(k + 1) * HD], (groups, HD))

    loads[0].wait()
    loads[1].wait()
    owner = lax.broadcasted_iota(jnp.int32, (rows, slots), 0) // groups
    lengths = jnp.zeros((rows, slots), jnp.int32)
    for i in range(n):
        lengths = jnp.where(owner == i, len_ref[i], lengths)
    live = lax.broadcasted_iota(jnp.int32, (rows, slots), 1) < lengths

    def own_head(k, carry):
        q = qsrc[k]
        s = jnp.zeros((rows, slots), F32)
        for i in range(n):
            part = lax.dot_general(q, sk[i, :, head_lanes(k)], NT, preferred_element_type=F32)
            s = jnp.where(owner == i, part, s)
        s = jnp.where(live, s * SCALE, -jnp.inf)
        own = jnp.sum(q32[k] * nk32[k], axis=1, keepdims=True) * SCALE
        top = jnp.maximum(jnp.max(s, axis=1, keepdims=True), own)
        wf = jnp.exp(s - top).astype(BF16).astype(F32)
        own_w = jnp.exp(own - top).astype(BF16).astype(F32)
        acc = own_w * nv32[k]
        for i in range(n):
            part = jnp.where(owner == i, wf, 0.0).astype(BF16)
            acc += jnp.dot(part, sv[i, :, head_lanes(k)], preferred_element_type=F32)
        lacc[k] = acc
        lm[k] = jnp.broadcast_to(top, (rows, HD))
        lmass[k] = jnp.broadcast_to(jnp.sum(wf, axis=1, keepdims=True) + own_w, (rows, HD))
        return carry

    lax.fori_loop(0, kv, own_head, 0)

    loads[2].wait()
    loads[3].wait()
    for swap in swaps:
        swap.wait_recv()
    each_peer(lambda r: q_copy(r, source(r)).wait_recv())
    chunks = [
        (b, pl.ds(c * KEY_CHUNK, KEY_CHUNK), pl.ds(b * prefix + c * KEY_CHUNK, KEY_CHUNK))
        for b in range(2) for c in range(prefix // KEY_CHUNK)
    ]
    lane = lax.broadcasted_iota(jnp.int32, (nb * rows, HD), 1)

    def prefix_head(k):
        lanes = pl.ds(k * HD, HD)
        q = qbuf[:, k].reshape(nb * rows, HD)
        fold = None
        for b, span, place in chunks:
            s = lax.dot_general(q, pk[b, span, lanes], NT, preferred_element_type=F32)
            sbuf[:, place] = s
            for p in range(KEY_CHUNK // HD):
                piece = s[:, p * HD:(p + 1) * HD]
                fold = piece if fold is None else jnp.maximum(fold, piece)
        top = (jnp.max(fold, axis=1, keepdims=True) * SCALE).astype(BF16).astype(F32)
        acc = jnp.zeros((nb * rows, HD), F32)
        total = jnp.zeros((nb * rows, HD), F32)
        for b, span, place in chunks:
            wb = jnp.exp(sbuf[:, place] * SCALE - top).astype(BF16)
            acc += jnp.dot(wb, pv[b, span, lanes], preferred_element_type=F32)
            wf = wb.astype(F32)
            for p in range(KEY_CHUNK // HD):
                total += wf[:, p * HD:(p + 1) * HD]
        mass = jnp.sum(total, axis=1, keepdims=True)
        high = mass.astype(BF16).astype(F32)
        stat = jnp.where(lane == 0, top, jnp.where(lane == 1, high, mass - high))
        psend[k, :, 0] = acc.astype(BF16).reshape(nb, rows, HD)
        psend[k, :, 1] = stat.astype(BF16).reshape(nb, rows, HD)

    for k in range(half):
        prefix_head(k)
        each_peer(functools.partial(lambda k, r: p_copy(k, r, me).start(), k))
        prec[k, me] = psend[k, me]

    def join(k):
        for p in range(2):
            h = p * half + k
            sources = range(p, nb, 2)
            stats = {j: prec[k, j, 1].astype(F32) for j in sources}
            tops = {j: jnp.broadcast_to(stats[j][:, :1], (rows, HD)) for j in sources}
            top = lm[h]
            for j in sources:
                top = jnp.maximum(top, tops[j])
            scale = jnp.exp(lm[h] - top)
            acc = lacc[h] * scale
            mass = lmass[h] * scale
            for j in sources:
                scale = jnp.exp(tops[j] - top)
                acc += prec[k, j, 0].astype(F32) * scale
                mass += scale * (stats[j][:, 1:2] + stats[j][:, 2:3])
            abuf[k, mb, p] = (acc / mass).astype(BF16)

    def a_copy(k, r, slot):
        return pltpu.make_async_remote_copy(
            src_ref=abuf.at[k, mb], dst_ref=abuf.at[k, slot],
            send_sem=a_s.at[k, r], recv_sem=a_r.at[k, r],
            device_id={"batch": lax.rem(mb + r, nbt)}, device_id_type=MESH,
        )

    part_rows = osend.shape[1]
    depth = groups * HD

    def project(k):
        for b in range(nbt):
            for p in range(2):
                h = p * half + k
                a32[b, h] = abuf[k, b, p].astype(F32)
                for g in range(groups):
                    x[b * n:(b + 1) * n, h * depth + g * HD:h * depth + (g + 1) * HD] = a32[
                        b, h, pl.ds(g, n, stride=groups), :
                    ]
        spans = [pl.ds((p * half + k) * depth, depth) for p in range(2)]
        xs = [x[:, span].astype(BF16) for span in spans]

        def column_block(c, carry):
            cols = pl.ds(pl.multiple_of(c * COL_CHUNK, COL_CHUNK), COL_CHUNK)
            part = jnp.dot(xs[0], w[spans[0], cols], preferred_element_type=F32)
            part += jnp.dot(xs[1], w[spans[1], cols], preferred_element_type=F32)
            for t in range(nt):
                piece = part[t * part_rows:(t + 1) * part_rows]
                osend[t, :, cols] = piece if k == 0 else osend[t, :, cols] + piece
            return carry

        lax.fori_loop(0, w.shape[1] // COL_CHUNK, column_block, 0)

    for k in range(half):
        each_peer(functools.partial(lambda k, r: p_copy(k, r, source(r)).wait_recv(), k))
        join(k)
        for r in range(1, nbt):
            a_copy(k, r, mb).start()
        if k > 0:
            for r in range(1, nbt):
                a_copy(k - 1, r, lax.rem(mb + nbt - r, nbt)).wait_recv()
            if k == 1:
                loads[4].wait()
            project(k - 1)
    for r in range(1, nbt):
        a_copy(half - 1, r, lax.rem(mb + nbt - r, nbt)).wait_recv()
    project(half - 1)

    def o_copy(r, slot):
        dst = lax.rem(mt + r, nt)
        return pltpu.make_async_remote_copy(
            src_ref=osend.at[dst], dst_ref=orecv.at[slot],
            send_sem=o_s.at[r], recv_sem=o_r.at[r],
            device_id={"tensor": dst}, device_id_type=MESH,
        )

    for r in range(1, nt):
        o_copy(r, mt).start()
    result = osend[mt]
    for r in range(1, nt):
        slot = lax.rem(mt + nt - r, nt)
        o_copy(r, slot).wait_recv()
        result = result + orecv[slot]
    o_ref[...] = result

    each_peer(lambda r: q_copy(r, me).wait_send())
    for k in range(half):
        each_peer(functools.partial(lambda k, r: p_copy(k, r, me).wait_send(), k))
        for r in range(1, nbt):
            a_copy(k, r, mb).wait_send()
    for swap in swaps:
        swap.wait_send()
    for r in range(1, nt):
        o_copy(r, mt).wait_send()


def body(
    nb, nbt, nt,
    queries, new_keys, new_values, suffix_keys, suffix_values, suffix_lengths,
    prefix_keys, prefix_values, out_weight,
):
    n = queries.shape[0]
    kv = new_keys.shape[-1] // HD
    groups = queries.shape[-1] // new_keys.shape[-1]
    rows = n * groups
    slots = suffix_keys.shape[1]
    cols = out_weight.shape[1]
    prefix = prefix_keys.shape[0]
    part_rows = nbt * n // nt
    half = kv // 2
    vmem = pl.BlockSpec(memory_space=pltpu.VMEM)
    smem = pl.BlockSpec(memory_space=pltpu.SMEM)
    hbm = pl.BlockSpec(memory_space=pl.ANY)
    dma = pltpu.SemaphoreType.DMA
    flops = 4 * nb * rows * prefix * HD * kv + 2 * nbt * n * out_weight.size
    return pl.pallas_call(
        functools.partial(kernel, nb, nbt, nt, n),
        out_shape=jax.ShapeDtypeStruct((part_rows, cols), F32),
        in_specs=[vmem] * 3 + [smem] + [hbm] * 5,
        out_specs=vmem,
        scratch_shapes=[
            pltpu.VMEM(suffix_keys.shape, BF16),
            pltpu.VMEM(suffix_values.shape, BF16),
            pltpu.VMEM((2, prefix, half * HD), BF16),
            pltpu.VMEM((2, prefix, half * HD), BF16),
            pltpu.VMEM(out_weight.shape, BF16),
            pltpu.VMEM((kv, rows, HD), F32),
            pltpu.VMEM((kv, rows, HD), F32),
            pltpu.VMEM((kv, rows, HD), F32),
            pltpu.VMEM((kv, rows, HD), BF16),
            pltpu.VMEM((nb, half, rows, HD), BF16),
            pltpu.VMEM((nb * rows, 2 * prefix), F32),
            pltpu.VMEM((half, nb, 2, rows, HD), BF16),
            pltpu.VMEM((half, nb, 2, rows, HD), BF16),
            pltpu.VMEM((kv, rows, HD), F32),
            pltpu.VMEM((kv, rows, HD), F32),
            pltpu.VMEM((kv, rows, HD), F32),
            pltpu.VMEM((half, nbt, 2, rows, HD), BF16),
            pltpu.VMEM((nbt, kv, rows, HD), F32),
            pltpu.VMEM((nbt * n, out_weight.shape[0]), F32),
            pltpu.VMEM((nt, part_rows, cols), F32),
            pltpu.VMEM((nt, part_rows, cols), F32),
            dma((5,)),
            dma((2,)), dma((2,)),
            dma((nb,)), dma((nb,)),
            dma((half, nb)), dma((half, nb)),
            dma((half, nbt)), dma((half, nbt)),
            dma((nt,)), dma((nt,)),
        ],
        compiler_params=pltpu.CompilerParams(
            collective_id=0, has_side_effects=True, vmem_limit_bytes=56 * 2**20
        ),
        cost_estimate=pl.CostEstimate(
            flops=flops,
            bytes_accessed=2 * (2 * suffix_keys.size + 2 * prefix_keys.size + out_weight.size),
            transcendentals=kv * rows * (nb * prefix + slots),
        ),
    )(queries, new_keys, new_values, suffix_lengths, suffix_keys, suffix_values,
      prefix_keys, prefix_values, out_weight).astype(BF16)


def solution(mesh):
    in_specs = (
        P(("blk", "batch"), "tensor"),
        P(("blk", "batch"), "tensor"),
        P(("blk", "batch"), "tensor"),
        P(("blk", "batch"), None, "tensor"),
        P(("blk", "batch"), None, "tensor"),
        P(("blk", "batch")),
        P("blk", "tensor"),
        P("blk", "tensor"),
        P("tensor", "batch"),
    )
    out_specs = P(("blk", "tensor"), "batch")
    sizes = (mesh.shape["blk"], mesh.shape["batch"], mesh.shape["tensor"])
    return jax.shard_map(
        functools.partial(body, *sizes), mesh=mesh, in_specs=in_specs, out_specs=out_specs,
        check_vma=False,
    )
```
